256 devices in a mesh: seq: 64 (over z, x, core), rate: 4 (over y).
Axes of the slice: x: 4, y: 4, z: 8, core: 2. Of those that a mesh axis runs over, the one named last changes fastest.
Arguments:
- projections: bfloat16 [8192, 3, 1536], P('seq'), may hold values from -10 to 10
- dilation_bits: int32 [4], P('rate'), may hold values from 0 to 3, as said below
- grad_out: bfloat16 [8192, 1536], P('seq'), may hold values from -6 to 6
Outputs:
- attended: bfloat16 [8192, 1536], P('seq', 'rate')
- grad_projections: bfloat16 [8192, 3, 1536], P('seq', None, 'rate')
The draws below stay inside these ranges and needn't reach their ends.
Inputs may be any that keep to these rules, and one draw needn't show every extreme that they name: `dilation_bits`: each entry is a whole number from 0 to 3; some branch has 3.
All inputs are finite; a program needn't handle non-finite values.
Results may differ from the reference program's by a relative error of at most 0.014.
Values may be sent and summed in bfloat16 or wider, within the bound.
No kernel may reach another device: no remote copies, remote signals or barrier semaphores. Data moves between devices by JAX's collectives and lax.ppermute only.
A program may use at most 128 MiB of HBM per device.

```python
import jax
import jax.numpy as jnp
from jax import lax

HEADS = 16
HEAD_DIM = 96
D = 1536
TOK_DEV = 128
MAX_BITS = 3
TOKENS = 8192
N_SEQ = 64
N_RATE = 4


def draw_projections(key, part):
    key = jax.random.fold_in(key, 5)
    factors = jnp.array([1.4, 1.4, 1.0], jnp.float32)[None, :, None]
    normal_draw = jax.random.truncated_normal(key, -4.0, 4.0, (TOKENS, 3, D), jnp.float32)
    return (normal_draw * factors).astype(jnp.bfloat16)


def draw_dilation_bits(key, part):
    key = jax.random.fold_in(key, 11)
    key_levels, key_high = jax.random.split(key, 2)
    levels = jax.random.randint(key_levels, (N_RATE,), 0, MAX_BITS + 1)
    high_slot = jax.random.randint(key_high, (), 0, N_RATE)
    branch_ids = jnp.arange(N_RATE)
    levels = jnp.where(branch_ids == high_slot, MAX_BITS, levels)
    return levels.astype(jnp.int32)


def block_levels(stream_key, extent, cuts, smallest, top_value):
    gain, own = 1.0, jax.random.fold_in(stream_key, 6)
    for dim, blocks in cuts:
        draws = jnp.exp(jax.random.uniform(jax.random.fold_in(own, dim), (blocks,), jnp.float32, smallest / len(cuts), top_value / len(cuts)))
        gain = gain * jnp.repeat(draws, extent[dim] // blocks).reshape([-1 if axis == dim else 1 for axis in range(len(extent))])
    return gain


def noise(own_key, dims, deviation, bound, cuts=(), held_as=jnp.bfloat16):
    values = deviation * jax.random.normal(own_key, dims, jnp.float32)
    if cuts:
        values = values * block_levels(own_key, dims, cuts, -0.22, 0.18)
    return jnp.clip(values, -bound, bound).astype(held_as)


def setup_inputs(seed: int = 0) -> dict:
    key_list = jax.random.split(jax.random.key(seed), 4)
    return {
        "projections": draw_projections(jax.random.fold_in(key_list[3], 71), 0),
        "dilation_bits": draw_dilation_bits(jax.random.fold_in(key_list[3], 71), 0),
        "grad_out": noise(key_list[2], (TOKENS, D), 1.0, 6.0, ((0, 64),)),
    }


def slot_tokens(dilation):
    stride = jnp.left_shift(jnp.int32(1), dilation).astype(jnp.int32)
    slots = jnp.arange(TOKENS, dtype=jnp.int32)
    groups = slots // TOK_DEV
    within = slots % TOK_DEV
    return ((groups // stride) * (TOK_DEV * stride) + within * stride + groups % stride).astype(jnp.int32)


def token_slots(dilation):
    stride = jnp.left_shift(jnp.int32(1), dilation).astype(jnp.int32)
    tokens = jnp.arange(TOKENS, dtype=jnp.int32)
    segment = TOK_DEV * stride
    inside = tokens % segment
    return (((tokens // segment) * stride + inside % stride) * TOK_DEV + inside // stride).astype(jnp.int32)


def attend_group(grouped):
    queries = grouped[:, 0].astype(jnp.float32)
    keyset = grouped[:, 1].astype(jnp.float32)
    valueset = grouped[:, 2].astype(jnp.float32)
    scores = jnp.einsum("qhd,khd->hqk", queries, keyset) * (HEAD_DIM ** -0.5)
    row_max = jnp.max(scores, axis=2, keepdims=True)
    exp_scores = jnp.exp(scores - row_max)
    row_sums = jnp.sum(exp_scores, axis=2)
    rounded = lax.optimization_barrier(exp_scores.astype(jnp.bfloat16)).astype(jnp.float32)
    weighted = jnp.einsum("hqk,khd->qhd", rounded, valueset)
    outputs = weighted / jnp.transpose(row_sums)[:, :, None]
    log_sums = jnp.transpose(row_max[:, :, 0] + jnp.log(row_sums))
    return outputs, log_sums


def grad_group(member):
    grouped, cotangent, log_total, inner_terms = member
    queries = grouped[:, 0].astype(jnp.float32)
    keyset = grouped[:, 1].astype(jnp.float32)
    valueset = grouped[:, 2].astype(jnp.float32)
    cot_rows = cotangent.astype(jnp.float32)
    score_scale = HEAD_DIM ** -0.5
    scores = jnp.einsum("qhd,khd->hqk", queries, keyset) * score_scale
    prob_rows = jnp.exp(scores - jnp.transpose(log_total)[:, :, None])
    prob_low = lax.optimization_barrier(prob_rows.astype(jnp.bfloat16)).astype(jnp.float32)
    grad_value = jnp.einsum("hqk,qhd->khd", prob_low, cot_rows)
    grad_prob = jnp.einsum("qhd,khd->hqk", cot_rows, valueset)
    grad_score = prob_rows * (grad_prob - jnp.transpose(inner_terms)[:, :, None])
    score_low = lax.optimization_barrier(grad_score.astype(jnp.bfloat16)).astype(jnp.float32)
    grad_query = jnp.einsum("hqk,khd->qhd", score_low, keyset) * score_scale
    grad_keyset = jnp.einsum("hqk,qhd->khd", score_low, queries) * score_scale
    return jnp.stack([grad_query, grad_keyset, grad_value], axis=1).astype(jnp.bfloat16)


def reference(projections, dilation_bits, grad_out):
    split_heads = projections.reshape(TOKENS, 3, HEADS, HEAD_DIM)
    branch_outs = []
    branch_lses = []
    for branch in range(N_RATE):
        slot_order = slot_tokens(dilation_bits[branch])
        back_order = token_slots(dilation_bits[branch])
        grouped = split_heads[slot_order].reshape(N_SEQ, TOK_DEV, 3, HEADS, HEAD_DIM)
        outputs, log_sums = lax.map(attend_group, grouped)
        branch_outs.append(outputs.reshape(TOKENS, HEADS, HEAD_DIM)[back_order])
        branch_lses.append(log_sums.reshape(TOKENS, HEADS)[back_order])
    row_max = branch_lses[0]
    for branch in range(1, N_RATE):
        row_max = jnp.maximum(row_max, branch_lses[branch])
    weight_sum = jnp.zeros((TOKENS, HEADS), jnp.float32)
    merged = jnp.zeros((TOKENS, HEADS, HEAD_DIM), jnp.float32)
    for branch in range(N_RATE):
        weight = jnp.exp(branch_lses[branch] - row_max)
        weight_sum = weight_sum + weight
        merged = merged + weight[:, :, None] * branch_outs[branch]
    merged = merged / weight_sum[:, :, None]
    lse_all = row_max + jnp.log(weight_sum)
    grad_heads = grad_out.reshape(TOKENS, HEADS, HEAD_DIM)
    inner_terms = jnp.sum(grad_heads.astype(jnp.float32) * merged, axis=2)
    grad_total = jnp.zeros((TOKENS, 3, HEADS, HEAD_DIM), jnp.float32)
    for branch in range(N_RATE):
        slot_order = slot_tokens(dilation_bits[branch])
        back_order = token_slots(dilation_bits[branch])
        grouped = split_heads[slot_order].reshape(N_SEQ, TOK_DEV, 3, HEADS, HEAD_DIM)
        cot_groups = grad_heads[slot_order].reshape(N_SEQ, TOK_DEV, HEADS, HEAD_DIM)
        lse_groups = lse_all[slot_order].reshape(N_SEQ, TOK_DEV, HEADS)
        inner_groups = inner_terms[slot_order].reshape(N_SEQ, TOK_DEV, HEADS)
        grad_groups = lax.map(grad_group, (grouped, cot_groups, lse_groups, inner_groups))
        grad_total = grad_total + grad_groups.reshape(TOKENS, 3, HEADS, HEAD_DIM)[back_order].astype(jnp.float32)
    attended = merged.reshape(TOKENS, D).astype(jnp.bfloat16)
    return attended, grad_total.reshape(TOKENS, 3, D).astype(jnp.bfloat16)
```

```python
import jax
import jax.numpy as jnp
from jax import lax
from jax.experimental import pallas as pl
from jax.experimental.pallas import tpu as pltpu
from jax.sharding import PartitionSpec as P

HEADS = 16
HEAD_DIM = 96
TOK = 128
CHIPS = 4
OWN = HEAD_DIM * HEADS // 4
TAIL = 128 - HEAD_DIM
SEG = 8 * TOK
HALF = 4 * TOK
NEG = -1e30
LOG2E = 1.4426950408889634
SCALE = HEAD_DIM ** -0.5
BF = jnp.bfloat16
F32 = jnp.float32
RATE_ON = ((0, 1, 0, 3), (0, 2, 0, 0))
BLOCK = 3 * TOK
NOTE = 16
WIDE = 256
VMEM_LIMIT = 48 * 1024 * 1024
PREP_LIMIT = 107 * 512 * 1024


def tiles(first, second, third, spread):
    parts = []
    for t, block in enumerate((first, second, third)):
        parts.append(jnp.concatenate([block, spread[:, t * TAIL : (t + 1) * TAIL]], axis=1))
    return jnp.concatenate(parts, axis=0)


def prep_kernel(bits, proj, cot, *rest):
    outs = rest[:CHIPS]
    proj_in, cot_in, sems = rest[CHIPS:]
    chip = chip_index()
    core = lax.axis_index("seq") & 1
    copies = []
    for d in range(CHIPS):
        head = lax.rem(chip + d, CHIPS)
        on = jnp.where(core == 0, RATE_ON[0][d], RATE_ON[1][d])
        rate = lax.rem(lax.axis_index("rate") + on, CHIPS)
        cols = pl.ds(pl.multiple_of(rate * OWN + (head // 2) * TOK, TOK), 2 * TOK)
        copies.append(
            [
                pltpu.make_async_copy(proj.at[:, :, cols], proj_in.at[d], sems.at[d, 0]),
                pltpu.make_async_copy(cot.at[:, cols], cot_in.at[d], sems.at[d, 1]),
            ]
        )
    for pair in copies:
        for copy in pair:
            copy.start()
    for pair in copies:
        for copy in pair:
            copy.wait()
    rate_row = jnp.full((NOTE, TOK), bits[0].astype(F32), F32).astype(BF)
    for d in range(CHIPS):
        outs[d][BLOCK:] = rate_row
    for at in range(CHIPS):

        @pl.when(chip == at)
        def _():
            for d in range(CHIPS):
                first = ((at + d) % CHIPS * HEAD_DIM, ((at + d) % CHIPS) // 2 * TOK)
                cols = slice(first[0] - first[1], first[0] - first[1] + HEAD_DIM)
                outs[d][:BLOCK] = tiles(
                    proj_in[d, 0, :, cols], proj_in[d, 1, :, cols], proj_in[d, 2, :, cols], cot_in[d, :, cols]
                )


def chip_index():
    return lax.rem(lax.axis_index("seq") // 2, CHIPS)


def prep(bits, proj, cot):
    hbm = pl.BlockSpec(memory_space=pltpu.HBM)
    return pl.pallas_call(
        prep_kernel,
        out_shape=[jax.ShapeDtypeStruct((BLOCK + NOTE, TOK), BF)] * CHIPS,
        in_specs=[pl.BlockSpec(memory_space=pltpu.SMEM), hbm, hbm],
        out_specs=[pl.BlockSpec(memory_space=pltpu.VMEM)] * CHIPS,
        scratch_shapes=[
            pltpu.VMEM((CHIPS, 3, TOK, 2 * TOK), BF),
            pltpu.VMEM((CHIPS, TOK, 2 * TOK), BF),
            pltpu.SemaphoreType.DMA((CHIPS, 2)),
        ],
        compiler_params=pltpu.CompilerParams(vmem_limit_bytes=PREP_LIMIT),
        name="prep",
    )(bits, proj, cot)


def main_kernel(*rest):
    ins = rest[:8]
    outs = rest[8:12]
    qs, ks, vs, ds, bias, st, dp, pt, gt = rest[12:]
    chip = chip_index()
    core = lax.axis_index("seq") & 1
    lane = lax.broadcasted_iota(jnp.int32, (TOK, TOK), 1)
    for s in range(8):
        rows = pl.ds(s * TOK, TOK)
        block = ins[s]
        qs[rows] = block[:TOK]
        ks[rows] = jnp.where(lane < HEAD_DIM, block[TOK : 2 * TOK], jnp.zeros((), BF))
        vs[rows] = block[2 * TOK : BLOCK]
        ds[rows] = jnp.concatenate(
            [block[t * TOK : (t + 1) * TOK, HEAD_DIM:] for t in range(3)] + [jnp.zeros((TOK, TAIL), BF)], axis=1
        )
    key = lax.broadcasted_iota(jnp.int32, (8, TOK), 0)
    query = lax.broadcasted_iota(jnp.int32, (8, TOK), 1) & 7
    apart = key ^ query
    count = jnp.zeros((8, TOK), F32)
    noted = [ins[0][BLOCK:].astype(F32)[:8]]
    for first, second in ((1, 5), (3, 7), (5, 1)):
        noted.append(jnp.where(core == 0, ins[first][BLOCK:].astype(F32)[:8], ins[second][BLOCK:].astype(F32)[:8]))
    for level, mask in ((0, 7), (1, 3), (2, 1), (3, 0)):
        rate_bits = 3 - level
        branches = jnp.zeros((8, TOK), F32)
        for b in range(4):
            branches = branches + jnp.where(noted[b] == float(rate_bits), 1.0, 0.0)
        count = count + jnp.where((apart & mask) == 0, branches, 0.0)
        bias[level] = jnp.where(count > 0.0, jnp.log2(jnp.maximum(count, 1.0)), NEG)

    odd = chip & 1
    nt = (((1,), (1,)), ((), ()))
    for c in range(SEG // WIDE):
        cols = slice(c * WIDE, (c + 1) * WIDE)
        st[...] = lax.dot_general(ks[...], qs[cols], nt, preferred_element_type=F32)
        dp[...] = lax.dot_general(vs[...], ds[cols], nt, preferred_element_type=F32)
        for i in range(c * WIDE // TOK, (c + 1) * WIDE // TOK):
            spot = slice(i * TOK - c * WIDE, (i + 1) * TOK - c * WIDE)
            cols = slice(i * TOK, (i + 1) * TOK)
            top = None
            di = i % 4
            for j in range(8):
                dj = j % 4
                if i == j:
                    level = 3
                elif di == dj:
                    level = 2
                elif dj == (3, 2, 1, 0)[di]:
                    level = 1 - odd
                elif dj == (1, 0, 3, 2)[di]:
                    level = odd
                else:
                    level = 0
                rows = slice(j * TOK, (j + 1) * TOK)
                t = st[rows, spot].reshape(16, 8, TOK) * (SCALE * LOG2E) + bias[level][None]
                st[rows, spot] = t.reshape(TOK, TOK)
                t_top = jnp.max(t, axis=0)
                top = t_top if top is None else jnp.maximum(top, t_top)
            top = jnp.max(top, axis=0, keepdims=True)
            total = jnp.zeros((8, TOK), F32)
            inner = jnp.zeros((8, TOK), F32)
            for j in range(8):
                rows = slice(j * TOK, (j + 1) * TOK)
                e = jnp.exp2(st[rows, spot] - top)
                st[rows, spot] = e
                e3 = e.reshape(16, 8, TOK)
                total = total + jnp.sum(e3, axis=0)
                inner = inner + jnp.sum(e3 * dp[rows, spot].reshape(16, 8, TOK), axis=0)
            over = 1.0 / jnp.sum(total, axis=0, keepdims=True)
            inner = jnp.sum(inner, axis=0, keepdims=True) * over
            for j in range(8):
                if i >= 4 and j >= 4:
                    continue
                rows = slice(j * TOK, (j + 1) * TOK)
                p = st[rows, spot] * over
                pt[rows, cols] = p.astype(BF)
                gt[rows, cols] = (p * (dp[rows, spot] - inner)).astype(BF)
    nn = (((1,), (0,)), ((), ()))
    tn = (((0,), (0,)), ((), ()))
    out = jnp.transpose(lax.dot_general(vs[...], pt[:, :HALF], tn, preferred_element_type=F32))
    gq = jnp.transpose(lax.dot_general(ks[...], gt[:, :HALF], tn, preferred_element_type=F32) * SCALE)
    gv = lax.dot_general(pt[:HALF], ds[...], nn, preferred_element_type=F32)
    gk = lax.dot_general(gt[:HALF], qs[...], nn, preferred_element_type=F32) * SCALE
    for d in range(4):
        rows = slice(d * TOK, (d + 1) * TOK)
        outs[d][...] = tiles(
            out[rows, :HEAD_DIM].astype(BF), gq[rows, :HEAD_DIM].astype(BF), gk[rows, :HEAD_DIM].astype(BF), gv[rows].astype(BF)
        )


def attend(blocks):
    vmem = pl.BlockSpec(memory_space=pltpu.VMEM)
    return pl.pallas_call(
        main_kernel,
        out_shape=[jax.ShapeDtypeStruct((BLOCK, TOK), BF)] * CHIPS,
        in_specs=[vmem] * 8,
        out_specs=[vmem] * CHIPS,
        scratch_shapes=[pltpu.VMEM((SEG, TOK), BF)] * 4
        + [
            pltpu.VMEM((4, 8, TOK), F32),
            pltpu.VMEM((SEG, WIDE), F32),
            pltpu.VMEM((SEG, WIDE), F32),
            pltpu.VMEM((SEG, SEG), BF),
            pltpu.VMEM((SEG, SEG), BF),
        ],
        compiler_params=pltpu.CompilerParams(vmem_limit_bytes=VMEM_LIMIT),
        name="attend",
    )(*blocks)


def final_kernel(*rest):
    ins = rest[:4]
    attended, grads, held = rest[4:]
    chip = chip_index()
    for d in range(CHIPS):
        held[lax.rem(chip + d, CHIPS)] = ins[d][...]
    for t in range(3):
        whole = jnp.concatenate([held[h, t * TOK : (t + 1) * TOK, :HEAD_DIM] for h in range(CHIPS)], axis=1)
        if t == 0:
            attended[...] = whole
        else:
            grads[t - 1] = whole
    grads[2] = jnp.concatenate(
        [held[h, t * TOK : (t + 1) * TOK, HEAD_DIM:] for h in range(CHIPS) for t in range(3)], axis=1
    )


def final(blocks):
    vmem = pl.BlockSpec(memory_space=pltpu.VMEM)
    return pl.pallas_call(
        final_kernel,
        out_shape=[jax.ShapeDtypeStruct((TOK, OWN), BF), jax.ShapeDtypeStruct((3, TOK, OWN), BF)],
        in_specs=[vmem] * 4,
        out_specs=[vmem] * 2,
        scratch_shapes=[pltpu.VMEM((CHIPS, BLOCK, TOK), BF)],
        compiler_params=pltpu.CompilerParams(vmem_limit_bytes=VMEM_LIMIT),
        name="final",
    )(*blocks)


def moved(block, chips, flip, rates):
    seq, ring = lax.axis_size("seq"), lax.axis_size("rate")
    pairs = []
    for i in range(seq):
        to = i - i % 8 + ((i // 2 + chips) % CHIPS) * 2 + (i % 2 ^ flip)
        for r in range(ring):
            pairs.append((i * ring + r, to * ring + (r + rates[i % 2]) % ring))
    return lax.ppermute(block, ("seq", "rate"), pairs)


def body(projections, dilation_bits, grad_out):
    sent = prep(dilation_bits, jnp.transpose(projections, (1, 0, 2)), grad_out)
    near = [sent[0]] + [moved(sent[d], d, 0, (RATE_ON[0][d], RATE_ON[1][d])) for d in range(1, CHIPS)]
    far = [moved(block, 0, 1, (0, 0)) for block in near]
    results = attend(near + far)
    back = [results[0]] + [moved(results[d], -d, 0, (0, 0)) for d in range(1, CHIPS)]
    attended, grads = final(back)
    return attended, jnp.transpose(grads, (1, 0, 2))


def solution(mesh):
    in_specs = (P("seq", None, None), P("rate"), P("seq", None))
    out_specs = (P("seq", "rate"), P("seq", None, "rate"))
    return jax.shard_map(body, mesh=mesh, in_specs=in_specs, out_specs=out_specs, check_vma=False)
```

```python
import jax
import jax.numpy as jnp
from jax import lax
from jax.experimental import pallas as pl
from jax.experimental.pallas import tpu as pltpu
from jax.sharding import PartitionSpec as P

HEADS = 16
HEAD_DIM = 96
TOK = 128
CHIPS = 4
OWN = HEAD_DIM * HEADS // 4
TAIL = 128 - HEAD_DIM
SEG = 8 * TOK
HALF = 4 * TOK
NEG = -1e30
LOG2E = 1.4426950408889634
SCALE = HEAD_DIM ** -0.5
TO_LOG2 = SCALE * LOG2E
BF = jnp.bfloat16
F32 = jnp.float32
MADE = ((0, (0, 0), True), (1, (1, 2), True), (2, (0, 0), False), (3, (0, 0), False), (0, (3, 3), True))
BLOCK = 3 * TOK
NOTE = 16
WIDE = 256
VMEM_LIMIT = 48 * 1024 * 1024
PREP_LIMIT = 213 * 256 * 1024


def tiles(first, second, third, spread):
    parts = []
    for t, block in enumerate((first, second, third)):
        parts.append(jnp.concatenate([block, spread[:, t * TAIL : (t + 1) * TAIL]], axis=1))
    return jnp.concatenate(parts, axis=0)


def prep_kernel(bits, proj, cot, *rest):
    outs = rest[: len(MADE)]
    proj_in, cot_in, sems = rest[len(MADE) :]
    chip = chip_index()
    core = lax.axis_index("seq") & 1
    copies = []
    for e, (step, on, _) in enumerate(MADE):
        head = lax.rem(chip + step, CHIPS)
        rate = lax.rem(lax.axis_index("rate") + jnp.where(core == 0, on[0], on[1]), CHIPS)
        cols = pl.ds(pl.multiple_of(rate * OWN + (head // 2) * TOK, TOK), 2 * TOK)
        copies.append(
            [
                pltpu.make_async_copy(proj.at[:, :, cols], proj_in.at[e], sems.at[e, 0]),
                pltpu.make_async_copy(cot.at[:, cols], cot_in.at[e], sems.at[e, 1]),
            ]
        )
    for pair in copies:
        for copy in pair:
            copy.start()
    note = jnp.full((NOTE, TOK), bits[0].astype(F32), F32).astype(BF)
    for e, (_, _, noted) in enumerate(MADE):
        if noted:
            outs[e][BLOCK:] = note
    for at in range(CHIPS):

        @pl.when(chip == at)
        def _():
            for e, (step, _, _) in enumerate(MADE):
                head = (at + step) % CHIPS
                first = head * HEAD_DIM - head // 2 * TOK
                cols = slice(first, first + HEAD_DIM)
                for copy in copies[e]:
                    copy.wait()
                outs[e][:BLOCK] = tiles(
                    proj_in[e, 0, :, cols], proj_in[e, 1, :, cols], proj_in[e, 2, :, cols], cot_in[e, :, cols]
                )


def chip_index():
    return lax.rem(lax.axis_index("seq") // 2, CHIPS)


def prep(bits, proj, cot):
    hbm = pl.BlockSpec(memory_space=pltpu.HBM)
    return pl.pallas_call(
        prep_kernel,
        out_shape=[jax.ShapeDtypeStruct((BLOCK + NOTE * noted, TOK), BF) for _, _, noted in MADE],
        in_specs=[pl.BlockSpec(memory_space=pltpu.SMEM), hbm, hbm],
        out_specs=[pl.BlockSpec(memory_space=pltpu.VMEM)] * len(MADE),
        scratch_shapes=[
            pltpu.VMEM((len(MADE), 3, TOK, 2 * TOK), BF),
            pltpu.VMEM((len(MADE), TOK, 2 * TOK), BF),
            pltpu.SemaphoreType.DMA((len(MADE), 2)),
        ],
        compiler_params=pltpu.CompilerParams(vmem_limit_bytes=PREP_LIMIT),
        name="prep",
    )(bits, proj, cot)


def near_level(i, j, odd):
    if i == j:
        return 3
    if i % 4 == j % 4:
        return 2
    if j % 4 == (3, 2, 1, 0)[i % 4]:
        return 1 - odd
    if j % 4 == (1, 0, 3, 2)[i % 4]:
        return odd
    return 0


def main_kernel(*rest):
    ins = rest[:8]
    outs = rest[8:12]
    qs, ks, vs, ds, bias, st, dp, et, gt, qn, dn, out, gq, gk, gv = rest[12:]
    odd = chip_index() & 1
    nn = (((1,), (0,)), ((), ()))
    nt = (((1,), (1,)), ((), ()))
    tn = (((0,), (0,)), ((), ()))
    lane = lax.broadcasted_iota(jnp.int32, (TOK, TOK), 1)
    for s in range(8):
        rows = pl.ds(s * TOK, TOK)
        block = ins[s]
        qs[rows] = block[:TOK]
        ks[rows] = jnp.where(lane < HEAD_DIM, block[TOK : 2 * TOK], jnp.zeros((), BF))
        vs[rows] = jnp.where(
            lane < HEAD_DIM, block[2 * TOK : BLOCK], jnp.where(lane == HEAD_DIM, jnp.ones((), BF), jnp.zeros((), BF))
        )
        ds[rows] = jnp.concatenate(
            [block[t * TOK : (t + 1) * TOK, HEAD_DIM:] for t in range(3)] + [jnp.zeros((TOK, TAIL), BF)], axis=1
        )
    key = lax.broadcasted_iota(jnp.int32, (8, TOK), 0)
    query = lax.broadcasted_iota(jnp.int32, (8, TOK), 1) & 7
    apart = key ^ query
    count = jnp.zeros((8, TOK), F32)
    noted = [ins[e][BLOCK:].astype(F32)[:8] for e in (0, 1, 4, 5)]
    for level, mask in ((0, 7), (1, 3), (2, 1), (3, 0)):
        rate_bits = 3 - level
        branches = jnp.zeros((8, TOK), F32)
        for b in range(4):
            branches = branches + jnp.where(noted[b] == float(rate_bits), 1.0, 0.0)
        count = count + jnp.where((apart & mask) == 0, branches, 0.0)
        bias[level] = jnp.where(count > 0.0, jnp.log2(jnp.maximum(count, 1.0)) * (1.0 / TO_LOG2), NEG)

    def products(c):
        cols = slice(c * WIDE, (c + 1) * WIDE)
        st[c] = lax.dot_general(ks[...], qs[cols], nt, preferred_element_type=F32)
        dp[c] = lax.dot_general(vs[...], ds[cols], nt, preferred_element_type=F32)

    def weights(c):
        for i in range(c * WIDE // TOK, (c + 1) * WIDE // TOK):
            spot = slice(i * TOK - c * WIDE, (i + 1) * TOK - c * WIDE)
            cols = slice(i * TOK, (i + 1) * TOK)
            near = [bias[near_level(i, j, odd)] for j in range(8)]
            top = None
            for j in range(8):
                rows = slice(j * TOK, (j + 1) * TOK)
                j_top = jnp.max(st[c, rows, spot].reshape(16, 8, TOK) + near[j][None], axis=0)
                top = j_top if top is None else jnp.maximum(top, j_top)
            top = jnp.max(top, axis=0, keepdims=True)
            for j in range(8):
                rows = slice(j * TOK, (j + 1) * TOK)
                t = st[c, rows, spot].reshape(16, 8, TOK) + (near[j] - top)[None]
                et[rows, cols] = jnp.exp2(t * TO_LOG2).reshape(TOK, TOK).astype(BF)

    def scores(c):
        cols = slice(c * WIDE, (c + 1) * WIDE)
        summed = lax.dot_general(vs[...], et[:, cols], tn, preferred_element_type=F32)
        over = 1.0 / summed[HEAD_DIM : HEAD_DIM + 1]
        merged = summed * over
        if c * WIDE < HALF:
            out[cols] = jnp.transpose(merged)
        inner = jnp.sum(merged * jnp.transpose(ds[cols].astype(F32)), axis=0, keepdims=True)
        for i in range(c * WIDE // TOK, (c + 1) * WIDE // TOK):
            spot = slice(i * TOK - c * WIDE, (i + 1) * TOK - c * WIDE)
            cols = slice(i * TOK, (i + 1) * TOK)
            for j in range(4 if i >= 4 else 8):
                rows = slice(j * TOK, (j + 1) * TOK)
                gt[rows, cols] = (et[rows, cols].astype(F32) * (dp[c, rows, spot] - inner[:, spot])).astype(BF)
            upright = jnp.transpose(jnp.broadcast_to(over[:, spot], (TOK, TOK)))
            qn[cols] = (qs[cols].astype(F32) * (upright * SCALE)).astype(BF)
            dn[cols] = (ds[cols].astype(F32) * upright).astype(BF)
        return over

    chunks = SEG // WIDE
    products(0)
    overs = []
    for c in range(chunks):
        if c + 1 < chunks:
            products(c + 1)
        weights(c)
        overs.append(scores(c))
    part = lax.dot_general(ks[...], gt[:, :HALF], tn, preferred_element_type=F32)
    gq[...] = jnp.transpose(part * (jnp.concatenate(overs[: HALF // WIDE], axis=1) * SCALE))
    gv[...] = lax.dot_general(et[:HALF], dn[...], nn, preferred_element_type=F32)
    gk[...] = lax.dot_general(gt[:HALF], qn[...], nn, preferred_element_type=F32)
    for d in range(4):
        rows = slice(d * TOK, (d + 1) * TOK)
        outs[d][...] = tiles(
            out[rows, :HEAD_DIM].astype(BF), gq[rows, :HEAD_DIM].astype(BF), gk[rows, :HEAD_DIM].astype(BF), gv[rows].astype(BF)
        )


def attend(blocks):
    vmem = pl.BlockSpec(memory_space=pltpu.VMEM)
    return pl.pallas_call(
        main_kernel,
        out_shape=[jax.ShapeDtypeStruct((BLOCK, TOK), BF)] * CHIPS,
        in_specs=[vmem] * 8,
        out_specs=[vmem] * CHIPS,
        scratch_shapes=[pltpu.VMEM((SEG, TOK), BF)] * 4
        + [
            pltpu.VMEM((4, 8, TOK), F32),
            pltpu.VMEM((SEG // WIDE, SEG, WIDE), F32),
            pltpu.VMEM((SEG // WIDE, SEG, WIDE), F32),
            pltpu.VMEM((SEG, SEG), BF),
            pltpu.VMEM((SEG, SEG), BF),
            pltpu.VMEM((SEG, TOK), BF),
            pltpu.VMEM((SEG, TOK), BF),
        ]
        + [pltpu.VMEM((HALF, TOK), F32)] * 4,
        compiler_params=pltpu.CompilerParams(vmem_limit_bytes=VMEM_LIMIT),
        name="attend",
    )(*blocks)


def final_kernel(*rest):
    ins = rest[:4]
    attended, grads, held, sems = rest[4:]
    chip = chip_index()
    copies = [pltpu.make_async_copy(held.at[0], attended, sems.at[0])]
    for t in range(3):
        copies.append(pltpu.make_async_copy(held.at[t + 1], grads.at[t], sems.at[t + 1]))
    for at in range(CHIPS):

        @pl.when(chip == at)
        def _():
            blocks = [ins[(h - at) % CHIPS] for h in range(CHIPS)]
            for t in range(3):
                held[t] = jnp.concatenate([block[t * TOK : (t + 1) * TOK, :HEAD_DIM] for block in blocks], axis=1)
                copies[t].start()
            held[3] = jnp.concatenate(
                [block[t * TOK : (t + 1) * TOK, HEAD_DIM:] for block in blocks for t in range(3)], axis=1
            )
            copies[3].start()

    for copy in copies:
        copy.wait()


def final(blocks):
    vmem = pl.BlockSpec(memory_space=pltpu.VMEM)
    hbm = pl.BlockSpec(memory_space=pltpu.HBM)
    return pl.pallas_call(
        final_kernel,
        out_shape=[jax.ShapeDtypeStruct((TOK, OWN), BF), jax.ShapeDtypeStruct((3, TOK, OWN), BF)],
        in_specs=[vmem] * 4,
        out_specs=[hbm] * 2,
        scratch_shapes=[pltpu.VMEM((4, TOK, OWN), BF), pltpu.SemaphoreType.DMA((4,))],
        compiler_params=pltpu.CompilerParams(vmem_limit_bytes=VMEM_LIMIT),
        name="final",
    )(*blocks)


def moved(block, chips, flip, rates):
    seq, ring = lax.axis_size("seq"), lax.axis_size("rate")
    pairs = []
    for i in range(seq):
        to = i - i % 8 + ((i // 2 + chips) % CHIPS) * 2 + (i % 2 ^ flip)
        for r in range(ring):
            pairs.append((i * ring + r, to * ring + (r + rates[i % 2]) % ring))
    return lax.ppermute(block, ("seq", "rate"), pairs)


def body(projections, dilation_bits, grad_out):
    sent = prep(dilation_bits, jnp.transpose(projections, (1, 0, 2)), grad_out)
    near = [sent[0]] + [moved(sent[e], MADE[e][0], 0, MADE[e][1]) for e in range(1, CHIPS)]
    far = [moved(sent[CHIPS], 0, 1, MADE[CHIPS][1])] + [moved(block, 0, 1, (0, 0)) for block in near[1:]]
    results = attend(near + far)
    back = [results[0]] + [moved(results[d], -d, 0, (0, 0)) for d in range(1, CHIPS)]
    attended, grads = final(back)
    return attended, jnp.transpose(grads, (1, 0, 2))


def solution(mesh):
    in_specs = (P("seq", None, None), P("rate"), P("seq", None))
    out_specs = (P("seq", "rate"), P("seq", None, "rate"))
    return jax.shard_map(body, mesh=mesh, in_specs=in_specs, out_specs=out_specs, check_vma=False)
```

```python
import jax
import jax.numpy as jnp
from jax import lax
from jax.experimental import pallas as pl
from jax.experimental.pallas import tpu as pltpu
from jax.sharding import PartitionSpec as P

HEADS = 16
HEAD_DIM = 96
TOK = 128
CHIPS = 4
OWN = HEAD_DIM * HEADS // 4
TAIL = 128 - HEAD_DIM
SEG = 8 * TOK
HALF = 4 * TOK
NEG = -1e30
LOG2E = 1.4426950408889634
SCALE = HEAD_DIM ** -0.5
TO_LOG2 = SCALE * LOG2E
BF = jnp.bfloat16
F32 = jnp.float32
MADE = ((0, (0, 0), True), (1, (1, 2), True), (2, (0, 0), False), (3, (0, 0), False), (0, (3, 3), True))
BACK = (0, 2, 3, 1)
BLOCK = 3 * TOK
NOTE = 16
WIDE = 256
VMEM_LIMIT = 48 * 1024 * 1024
PREP_LIMIT = 213 * 256 * 1024


def tiles(first, second, third, spread):
    parts = []
    for t, block in enumerate((first, second, third)):
        parts.append(jnp.concatenate([block, spread[:, t * TAIL : (t + 1) * TAIL]], axis=1))
    return jnp.concatenate(parts, axis=0)


def prep_kernel(bits, proj, cot, *rest):
    outs = rest[: len(MADE)]
    proj_in, cot_in, sems = rest[len(MADE) :]
    chip = chip_index()
    core = lax.axis_index("seq") & 1
    copies = []
    for e, (step, on, _) in enumerate(MADE):
        head = lax.rem(chip + step, CHIPS)
        rate = lax.rem(lax.axis_index("rate") + jnp.where(core == 0, on[0], on[1]), CHIPS)
        cols = pl.ds(pl.multiple_of(rate * OWN + (head // 2) * TOK, TOK), 2 * TOK)
        copies.append(
            [
                pltpu.make_async_copy(proj.at[:, :, cols], proj_in.at[e], sems.at[e, 0]),
                pltpu.make_async_copy(cot.at[:, cols], cot_in.at[e], sems.at[e, 1]),
            ]
        )
    for pair in copies:
        for copy in pair:
            copy.start()
    note = jnp.full((NOTE, TOK), bits[0].astype(F32), F32).astype(BF)
    for e, (_, _, noted) in enumerate(MADE):
        if noted:
            outs[e][BLOCK:] = note
    for at in range(CHIPS):

        @pl.when(chip == at)
        def _():
            for e, (step, _, _) in enumerate(MADE):
                head = (at + step) % CHIPS
                first = head * HEAD_DIM - head // 2 * TOK
                cols = slice(first, first + HEAD_DIM)
                for copy in copies[e]:
                    copy.wait()
                outs[e][:BLOCK] = tiles(
                    proj_in[e, 0, :, cols], proj_in[e, 1, :, cols], proj_in[e, 2, :, cols], cot_in[e, :, cols]
                )


def chip_index():
    return lax.rem(lax.axis_index("seq") // 2, CHIPS)


def prep(bits, proj, cot):
    hbm = pl.BlockSpec(memory_space=pltpu.HBM)
    return pl.pallas_call(
        prep_kernel,
        out_shape=[jax.ShapeDtypeStruct((BLOCK + NOTE * noted, TOK), BF) for _, _, noted in MADE],
        in_specs=[pl.BlockSpec(memory_space=pltpu.SMEM), hbm, hbm],
        out_specs=[pl.BlockSpec(memory_space=pltpu.VMEM)] * len(MADE),
        scratch_shapes=[
            pltpu.VMEM((len(MADE), 3, TOK, 2 * TOK), BF),
            pltpu.VMEM((len(MADE), TOK, 2 * TOK), BF),
            pltpu.SemaphoreType.DMA((len(MADE), 2)),
        ],
        compiler_params=pltpu.CompilerParams(vmem_limit_bytes=PREP_LIMIT),
        name="prep",
    )(bits, proj, cot)


def near_level(i, j, odd):
    if i == j:
        return 3
    if i % 4 == j % 4:
        return 2
    if j % 4 == (3, 2, 1, 0)[i % 4]:
        return 1 - odd
    if j % 4 == (1, 0, 3, 2)[i % 4]:
        return odd
    return 0


def main_kernel(*rest):
    ins = rest[:8]
    outs = rest[8:12]
    qs, ks, vs, ds, bias, st, dp, et, gt, qn, dn, out, gq, gk, gv = rest[12:]
    odd = chip_index() & 1
    nn = (((1,), (0,)), ((), ()))
    nt = (((1,), (1,)), ((), ()))
    tn = (((0,), (0,)), ((), ()))
    lane = lax.broadcasted_iota(jnp.int32, (TOK, TOK), 1)
    for s in range(8):
        rows = pl.ds(s * TOK, TOK)
        block = ins[s]
        qs[rows] = block[:TOK]
        ks[rows] = jnp.where(lane < HEAD_DIM, block[TOK : 2 * TOK], jnp.zeros((), BF))
        vs[rows] = jnp.where(
            lane < HEAD_DIM, block[2 * TOK : BLOCK], jnp.where(lane == HEAD_DIM, jnp.ones((), BF), jnp.zeros((), BF))
        )
        ds[rows] = jnp.concatenate(
            [block[t * TOK : (t + 1) * TOK, HEAD_DIM:] for t in range(3)] + [jnp.zeros((TOK, TAIL), BF)], axis=1
        )
    key = lax.broadcasted_iota(jnp.int32, (8, TOK), 0)
    query = lax.broadcasted_iota(jnp.int32, (8, TOK), 1) & 7
    apart = key ^ query
    count = jnp.zeros((8, TOK), F32)
    noted = [ins[e][BLOCK:].astype(F32)[:8] for e in (0, 1, 4, 5)]
    for level, mask in ((0, 7), (1, 3), (2, 1), (3, 0)):
        rate_bits = 3 - level
        branches = jnp.zeros((8, TOK), F32)
        for b in range(4):
            branches = branches + jnp.where(noted[b] == float(rate_bits), 1.0, 0.0)
        count = count + jnp.where((apart & mask) == 0, branches, 0.0)
        bias[level] = jnp.where(count > 0.0, jnp.log2(jnp.maximum(count, 1.0)) * (1.0 / TO_LOG2), NEG)

    def products(c):
        cols = slice(c * WIDE, (c + 1) * WIDE)
        st[c] = lax.dot_general(ks[...], qs[cols], nt, preferred_element_type=F32)
        dp[c] = lax.dot_general(vs[...], ds[cols], nt, preferred_element_type=F32)

    def weights(c):
        for i in range(c * WIDE // TOK, (c + 1) * WIDE // TOK):
            spot = slice(i * TOK - c * WIDE, (i + 1) * TOK - c * WIDE)
            cols = slice(i * TOK, (i + 1) * TOK)
            near = [bias[near_level(i, j, odd)] for j in range(8)]
            top = None
            for j in range(8):
                rows = slice(j * TOK, (j + 1) * TOK)
                j_top = jnp.max(st[c, rows, spot].reshape(16, 8, TOK) + near[j][None], axis=0)
                top = j_top if top is None else jnp.maximum(top, j_top)
            top = jnp.max(top, axis=0, keepdims=True)
            for j in range(8):
                rows = slice(j * TOK, (j + 1) * TOK)
                t = st[c, rows, spot].reshape(16, 8, TOK) + (near[j] - top)[None]
                et[rows, cols] = jnp.exp2(t * TO_LOG2).reshape(TOK, TOK).astype(BF)

    def scores(c):
        cols = slice(c * WIDE, (c + 1) * WIDE)
        summed = lax.dot_general(vs[...], et[:, cols], tn, preferred_element_type=F32)
        over = 1.0 / summed[HEAD_DIM : HEAD_DIM + 1]
        merged = summed * over
        if c * WIDE < HALF:
            out[cols] = jnp.transpose(merged)
        inner = jnp.sum(merged * jnp.transpose(ds[cols].astype(F32)), axis=0, keepdims=True)
        for i in range(c * WIDE // TOK, (c + 1) * WIDE // TOK):
            spot = slice(i * TOK - c * WIDE, (i + 1) * TOK - c * WIDE)
            cols = slice(i * TOK, (i + 1) * TOK)
            for j in range(4 if i >= 4 else 8):
                rows = slice(j * TOK, (j + 1) * TOK)
                gt[rows, cols] = (et[rows, cols].astype(F32) * (dp[c, rows, spot] - inner[:, spot])).astype(BF)
            upright = jnp.transpose(jnp.broadcast_to(over[:, spot], (TOK, TOK)))
            qn[cols] = (qs[cols].astype(F32) * (upright * SCALE)).astype(BF)
            dn[cols] = (ds[cols].astype(F32) * upright).astype(BF)
        return over

    chunks = SEG // WIDE
    products(0)
    overs = []
    for c in range(chunks):
        if c + 1 < chunks:
            products(c + 1)
        weights(c)
        overs.append(scores(c))
    part = lax.dot_general(ks[...], gt[:, :HALF], tn, preferred_element_type=F32)
    gq[...] = jnp.transpose(part * (jnp.concatenate(overs[: HALF // WIDE], axis=1) * SCALE))
    gv[...] = lax.dot_general(et[:HALF], dn[...], nn, preferred_element_type=F32)
    gk[...] = lax.dot_general(gt[:HALF], qn[...], nn, preferred_element_type=F32)
    made = []
    for d in range(4):
        rows = slice(d * TOK, (d + 1) * TOK)
        made.append(
            tiles(
                out[rows, :HEAD_DIM].astype(BF),
                gq[rows, :HEAD_DIM].astype(BF),
                gk[rows, :HEAD_DIM].astype(BF),
                gv[rows].astype(BF),
            )
        )
    outs[0][...] = made[0]
    outs[1][...] = jnp.where(odd == 1, made[1], made[3])
    outs[2][...] = made[2]
    outs[3][...] = jnp.where(odd == 1, made[3], made[1])


def attend(blocks):
    vmem = pl.BlockSpec(memory_space=pltpu.VMEM)
    return pl.pallas_call(
        main_kernel,
        out_shape=[jax.ShapeDtypeStruct((BLOCK, TOK), BF)] * CHIPS,
        in_specs=[vmem] * 8,
        out_specs=[vmem] * CHIPS,
        scratch_shapes=[pltpu.VMEM((SEG, TOK), BF)] * 4
        + [
            pltpu.VMEM((4, 8, TOK), F32),
            pltpu.VMEM((SEG // WIDE, SEG, WIDE), F32),
            pltpu.VMEM((SEG // WIDE, SEG, WIDE), F32),
            pltpu.VMEM((SEG, SEG), BF),
            pltpu.VMEM((SEG, SEG), BF),
            pltpu.VMEM((SEG, TOK), BF),
            pltpu.VMEM((SEG, TOK), BF),
        ]
        + [pltpu.VMEM((HALF, TOK), F32)] * 4,
        compiler_params=pltpu.CompilerParams(vmem_limit_bytes=VMEM_LIMIT),
        name="attend",
    )(*blocks)


def final_kernel(*rest):
    ins = rest[:4]
    attended, grads, held, sems = rest[4:]
    chip = chip_index()
    copies = [pltpu.make_async_copy(held.at[0], attended, sems.at[0])]
    for t in range(3):
        copies.append(pltpu.make_async_copy(held.at[t + 1], grads.at[t], sems.at[t + 1]))
    for at in range(CHIPS):

        @pl.when(chip == at)
        def _():
            blocks = [ins[BACK.index(h ^ at)] for h in range(CHIPS)]
            for t in range(3):
                held[t] = jnp.concatenate([block[t * TOK : (t + 1) * TOK, :HEAD_DIM] for block in blocks], axis=1)
                copies[t].start()
            held[3] = jnp.concatenate(
                [block[t * TOK : (t + 1) * TOK, HEAD_DIM:] for block in blocks for t in range(3)], axis=1
            )
            copies[3].start()

    for copy in copies:
        copy.wait()


def final(blocks):
    vmem = pl.BlockSpec(memory_space=pltpu.VMEM)
    hbm = pl.BlockSpec(memory_space=pltpu.HBM)
    return pl.pallas_call(
        final_kernel,
        out_shape=[jax.ShapeDtypeStruct((TOK, OWN), BF), jax.ShapeDtypeStruct((3, TOK, OWN), BF)],
        in_specs=[vmem] * 4,
        out_specs=[hbm] * 2,
        scratch_shapes=[pltpu.VMEM((4, TOK, OWN), BF), pltpu.SemaphoreType.DMA((4,))],
        compiler_params=pltpu.CompilerParams(vmem_limit_bytes=VMEM_LIMIT),
        name="final",
    )(*blocks)


def moved(block, chips, flip, rates):
    seq, ring = lax.axis_size("seq"), lax.axis_size("rate")
    pairs = []
    for i in range(seq):
        to = i - i % 8 + ((i // 2 + chips) % CHIPS) * 2 + (i % 2 ^ flip)
        for r in range(ring):
            pairs.append((i * ring + r, to * ring + (r + rates[i % 2]) % ring))
    return lax.ppermute(block, ("seq", "rate"), pairs)


def traded(block, across):
    return lax.ppermute(block, "seq", [(i, i ^ across * 2) for i in range(lax.axis_size("seq"))])


def body(projections, dilation_bits, grad_out):
    sent = prep(dilation_bits, jnp.transpose(projections, (1, 0, 2)), grad_out)
    near = [sent[0]] + [moved(sent[e], MADE[e][0], 0, MADE[e][1]) for e in range(1, CHIPS)]
    far = [moved(sent[CHIPS], 0, 1, MADE[CHIPS][1])] + [moved(block, 0, 1, (0, 0)) for block in near[1:]]
    results = attend(near + far)
    back = [traded(results[k], k) if k else results[k] for k in BACK]
    attended, grads = final(back)
    return attended, jnp.transpose(grads, (1, 0, 2))


def solution(mesh):
    in_specs = (P("seq", None, None), P("rate"), P("seq", None))
    out_specs = (P("seq", "rate"), P("seq", None, "rate"))
    return jax.shard_map(body, mesh=mesh, in_specs=in_specs, out_specs=out_specs, check_vma=False)
```

```python
import jax
import jax.numpy as jnp
from jax import lax
from jax.experimental import pallas as pl
from jax.experimental.pallas import tpu as pltpu
from jax.sharding import PartitionSpec as P

HEADS = 16
HEAD_DIM = 96
TOK = 128
CHIPS = 4
OWN = HEAD_DIM * HEADS // 4
TAIL = 128 - HEAD_DIM
SEG = 8 * TOK
HALF = 4 * TOK
NEG = -1e30
LOG2E = 1.4426950408889634
SCALE = HEAD_DIM ** -0.5
TO_LOG2 = SCALE * LOG2E
BF = jnp.bfloat16
F32 = jnp.float32
MADE = ((0, (0, 0), True), (1, (1, 2), True), (2, (0, 0), False), (3, (0, 0), False), (0, (3, 3), True))
BACK = (0, 2, 3, 1)
BLOCK = 3 * TOK
NOTE = 16
WIDE = 256
VMEM_LIMIT = 48 * 1024 * 1024
PREP_LIMIT = 213 * 256 * 1024


def tiles(first, second, third, spread):
    parts = []
    for t, block in enumerate((first, second, third)):
        parts.append(jnp.concatenate([block, spread[:, t * TAIL : (t + 1) * TAIL]], axis=1))
    return jnp.concatenate(parts, axis=0)


def prep_kernel(bits, proj, cot, *rest):
    outs = rest[: len(MADE)]
    proj_in, cot_in, sems = rest[len(MADE) :]
    chip = chip_index()
    core = lax.axis_index("seq") & 1
    copies = []
    for e, (step, on, _) in enumerate(MADE):
        head = lax.rem(chip + step, CHIPS)
        rate = lax.rem(lax.axis_index("rate") + jnp.where(core == 0, on[0], on[1]), CHIPS)
        cols = pl.ds(pl.multiple_of(rate * OWN + (head // 2) * TOK, TOK), 2 * TOK)
        copies.append(
            [
                pltpu.make_async_copy(proj.at[:, :, cols], proj_in.at[e], sems.at[e, 0]),
                pltpu.make_async_copy(cot.at[:, cols], cot_in.at[e], sems.at[e, 1]),
            ]
        )
    for pair in copies:
        for copy in pair:
            copy.start()
    note = jnp.full((NOTE, TOK), bits[0].astype(F32), F32).astype(BF)
    for e, (_, _, noted) in enumerate(MADE):
        if noted:
            outs[e][BLOCK:] = note
    for at in range(CHIPS):

        @pl.when(chip == at)
        def _():
            for e, (step, _, _) in enumerate(MADE):
                head = (at + step) % CHIPS
                first = head * HEAD_DIM - head // 2 * TOK
                cols = slice(first, first + HEAD_DIM)
                for copy in copies[e]:
                    copy.wait()
                outs[e][:BLOCK] = tiles(
                    proj_in[e, 0, :, cols], proj_in[e, 1, :, cols], proj_in[e, 2, :, cols], cot_in[e, :, cols]
                )


def chip_index():
    return lax.rem(lax.axis_index("seq") // 2, CHIPS)


def prep(bits, proj, cot):
    hbm = pl.BlockSpec(memory_space=pltpu.HBM)
    return pl.pallas_call(
        prep_kernel,
        out_shape=[jax.ShapeDtypeStruct((BLOCK + NOTE * noted, TOK), BF) for _, _, noted in MADE],
        in_specs=[pl.BlockSpec(memory_space=pltpu.SMEM), hbm, hbm],
        out_specs=[pl.BlockSpec(memory_space=pltpu.VMEM)] * len(MADE),
        scratch_shapes=[
            pltpu.VMEM((len(MADE), 3, TOK, 2 * TOK), BF),
            pltpu.VMEM((len(MADE), TOK, 2 * TOK), BF),
            pltpu.SemaphoreType.DMA((len(MADE), 2)),
        ],
        compiler_params=pltpu.CompilerParams(vmem_limit_bytes=PREP_LIMIT),
        name="prep",
    )(bits, proj, cot)


def near_level(i, j, odd):
    if i == j:
        return 3
    if i % 4 == j % 4:
        return 2
    if j % 4 == (3, 2, 1, 0)[i % 4]:
        return 1 - odd
    if j % 4 == (1, 0, 3, 2)[i % 4]:
        return odd
    return 0


def main_kernel(*rest):
    ins = rest[:8]
    outs = rest[8:12]
    qs, ks, vs, ds, bias, st, dp, et, gt, qn, dn, out, gq, gk, gv = rest[12:]
    odd = chip_index() & 1
    nn = (((1,), (0,)), ((), ()))
    nt = (((1,), (1,)), ((), ()))
    tn = (((0,), (0,)), ((), ()))
    lane = lax.broadcasted_iota(jnp.int32, (TOK, TOK), 1)
    for s in range(8):
        rows = pl.ds(s * TOK, TOK)
        block = ins[s]
        qs[rows] = block[:TOK]
        ks[rows] = jnp.where(lane < HEAD_DIM, block[TOK : 2 * TOK], jnp.zeros((), BF))
        vs[rows] = jnp.where(
            lane < HEAD_DIM, block[2 * TOK : BLOCK], jnp.where(lane == HEAD_DIM, jnp.ones((), BF), jnp.zeros((), BF))
        )
        ds[rows] = jnp.concatenate(
            [block[t * TOK : (t + 1) * TOK, HEAD_DIM:] for t in range(3)] + [jnp.zeros((TOK, TAIL), BF)], axis=1
        )
    key = lax.broadcasted_iota(jnp.int32, (8, TOK), 0)
    query = lax.broadcasted_iota(jnp.int32, (8, TOK), 1) & 7
    apart = key ^ query
    count = jnp.zeros((8, TOK), F32)
    noted = [ins[e][BLOCK:].astype(F32)[:8] for e in (0, 1, 4, 5)]
    for level, mask in ((0, 7), (1, 3), (2, 1), (3, 0)):
        rate_bits = 3 - level
        branches = jnp.zeros((8, TOK), F32)
        for b in range(4):
            branches = branches + jnp.where(noted[b] == float(rate_bits), 1.0, 0.0)
        count = count + jnp.where((apart & mask) == 0, branches, 0.0)
        bias[level] = jnp.where(count > 0.0, jnp.log2(jnp.maximum(count, 1.0)) * (1.0 / TO_LOG2), NEG)

    def products(c):
        cols = slice(c * WIDE, (c + 1) * WIDE)
        st[c] = lax.dot_general(ks[...], qs[cols], nt, preferred_element_type=F32)
        keys = slice(0, SEG if c * WIDE < HALF else HALF)
        dp[c, keys] = lax.dot_general(vs[keys], ds[cols], nt, preferred_element_type=F32)

    def weights(c):
        for i in range(c * WIDE // TOK, (c + 1) * WIDE // TOK):
            spot = slice(i * TOK - c * WIDE, (i + 1) * TOK - c * WIDE)
            cols = slice(i * TOK, (i + 1) * TOK)
            near = [bias[near_level(i, j, odd)] for j in range(8)]
            top = None
            for j in range(8):
                rows = slice(j * TOK, (j + 1) * TOK)
                j_top = jnp.max(st[c, rows, spot].reshape(16, 8, TOK) + near[j][None], axis=0)
                top = j_top if top is None else jnp.maximum(top, j_top)
            top = jnp.max(top, axis=0, keepdims=True)
            for j in range(8):
                rows = slice(j * TOK, (j + 1) * TOK)
                t = st[c, rows, spot].reshape(16, 8, TOK) + (near[j] - top)[None]
                et[rows, cols] = jnp.exp2(t * TO_LOG2).reshape(TOK, TOK).astype(BF)

    def scores(c):
        cols = slice(c * WIDE, (c + 1) * WIDE)
        summed = lax.dot_general(vs[...], et[:, cols], tn, preferred_element_type=F32)
        over = 1.0 / summed[HEAD_DIM : HEAD_DIM + 1]
        merged = summed * over
        if c * WIDE < HALF:
            out[cols] = jnp.transpose(merged)
        inner = jnp.sum(merged * jnp.transpose(ds[cols].astype(F32)), axis=0, keepdims=True)
        for i in range(c * WIDE // TOK, (c + 1) * WIDE // TOK):
            spot = slice(i * TOK - c * WIDE, (i + 1) * TOK - c * WIDE)
            cols = slice(i * TOK, (i + 1) * TOK)
            for j in range(4 if i >= 4 else 8):
                rows = slice(j * TOK, (j + 1) * TOK)
                gt[rows, cols] = (et[rows, cols].astype(F32) * (dp[c, rows, spot] - inner[:, spot])).astype(BF)
            upright = jnp.transpose(jnp.broadcast_to(over[:, spot], (TOK, TOK)))
            qn[cols] = (qs[cols].astype(F32) * (upright * SCALE)).astype(BF)
            dn[cols] = (ds[cols].astype(F32) * upright).astype(BF)
        return over

    chunks = SEG // WIDE
    products(0)
    overs = []
    for c in range(chunks):
        if c + 1 < chunks:
            products(c + 1)
        weights(c)
        overs.append(scores(c))
    gv[...] = lax.dot_general(et[:HALF], dn[...], nn, preferred_element_type=F32)
    gk[...] = lax.dot_general(gt[:HALF], qn[...], nn, preferred_element_type=F32)
    part = lax.dot_general(ks[...], gt[:, :HALF], tn, preferred_element_type=F32)
    gq[...] = jnp.transpose(part * (jnp.concatenate(overs[: HALF // WIDE], axis=1) * SCALE))
    made = []
    for d in range(4):
        rows = slice(d * TOK, (d + 1) * TOK)
        made.append(
            tiles(
                out[rows, :HEAD_DIM].astype(BF),
                gq[rows, :HEAD_DIM].astype(BF),
                gk[rows, :HEAD_DIM].astype(BF),
                gv[rows].astype(BF),
            )
        )
    outs[0][...] = made[0]
    outs[1][...] = jnp.where(odd == 1, made[1], made[3])
    outs[2][...] = made[2]
    outs[3][...] = jnp.where(odd == 1, made[3], made[1])


def attend(blocks):
    vmem = pl.BlockSpec(memory_space=pltpu.VMEM)
    return pl.pallas_call(
        main_kernel,
        out_shape=[jax.ShapeDtypeStruct((BLOCK, TOK), BF)] * CHIPS,
        in_specs=[vmem] * 8,
        out_specs=[vmem] * CHIPS,
        scratch_shapes=[pltpu.VMEM((SEG, TOK), BF)] * 4
        + [
            pltpu.VMEM((4, 8, TOK), F32),
            pltpu.VMEM((SEG // WIDE, SEG, WIDE), F32),
            pltpu.VMEM((SEG // WIDE, SEG, WIDE), F32),
            pltpu.VMEM((SEG, SEG), BF),
            pltpu.VMEM((SEG, SEG), BF),
            pltpu.VMEM((SEG, TOK), BF),
            pltpu.VMEM((SEG, TOK), BF),
        ]
        + [pltpu.VMEM((HALF, TOK), F32)] * 4,
        compiler_params=pltpu.CompilerParams(vmem_limit_bytes=VMEM_LIMIT),
        name="attend",
    )(*blocks)


def final_kernel(*rest):
    ins = rest[:4]
    attended, grads, held, sems = rest[4:]
    chip = chip_index()
    copies = [pltpu.make_async_copy(held.at[0], attended, sems.at[0])]
    for t in range(3):
        copies.append(pltpu.make_async_copy(held.at[t + 1], grads.at[t], sems.at[t + 1]))
    for at in range(CHIPS):

        @pl.when(chip == at)
        def _():
            blocks = [ins[BACK.index(h ^ at)] for h in range(CHIPS)]
            for t in range(3):
                held[t] = jnp.concatenate([block[t * TOK : (t + 1) * TOK, :HEAD_DIM] for block in blocks], axis=1)
                copies[t].start()
            held[3] = jnp.concatenate(
                [block[t * TOK : (t + 1) * TOK, HEAD_DIM:] for block in blocks for t in range(3)], axis=1
            )
            copies[3].start()

    for copy in copies:
        copy.wait()


def final(blocks):
    vmem = pl.BlockSpec(memory_space=pltpu.VMEM)
    hbm = pl.BlockSpec(memory_space=pltpu.HBM)
    return pl.pallas_call(
        final_kernel,
        out_shape=[jax.ShapeDtypeStruct((TOK, OWN), BF), jax.ShapeDtypeStruct((3, TOK, OWN), BF)],
        in_specs=[vmem] * 4,
        out_specs=[hbm] * 2,
        scratch_shapes=[pltpu.VMEM((4, TOK, OWN), BF), pltpu.SemaphoreType.DMA((4,))],
        compiler_params=pltpu.CompilerParams(vmem_limit_bytes=VMEM_LIMIT),
        name="final",
    )(*blocks)


def moved(block, chips, flip, rates):
    seq, ring = lax.axis_size("seq"), lax.axis_size("rate")
    pairs = []
    for i in range(seq):
        to = i - i % 8 + ((i // 2 + chips) % CHIPS) * 2 + (i % 2 ^ flip)
        for r in range(ring):
            pairs.append((i * ring + r, to * ring + (r + rates[i % 2]) % ring))
    return lax.ppermute(block, ("seq", "rate"), pairs)


def traded(block, across):
    return lax.ppermute(block, "seq", [(i, i ^ across * 2) for i in range(lax.axis_size("seq"))])


def body(projections, dilation_bits, grad_out):
    sent = prep(dilation_bits, jnp.transpose(projections, (1, 0, 2)), grad_out)
    near = [sent[0]] + [moved(sent[e], MADE[e][0], 0, MADE[e][1]) for e in range(1, CHIPS)]
    far = [moved(sent[CHIPS], 0, 1, MADE[CHIPS][1])] + [moved(block, 0, 1, (0, 0)) for block in near[1:]]
    results = attend(near + far)
    back = [traded(results[k], k) if k else results[k] for k in BACK]
    attended, grads = final(back)
    return attended, jnp.transpose(grads, (1, 0, 2))


def solution(mesh):
    in_specs = (P("seq", None, None), P("rate"), P("seq", None))
    out_specs = (P("seq", "rate"), P("seq", None, "rate"))
    return jax.shard_map(body, mesh=mesh, in_specs=in_specs, out_specs=out_specs, check_vma=False)
```

```python
import jax
import jax.numpy as jnp
from jax import lax
from jax.experimental import pallas as pl
from jax.experimental.pallas import tpu as pltpu
from jax.sharding import PartitionSpec as P

HEADS = 16
HEAD_DIM = 96
TOK = 128
CHIPS = 4
OWN = HEAD_DIM * HEADS // 4
TAIL = 128 - HEAD_DIM
SEG = 8 * TOK
HALF = 4 * TOK
NEG = -1e30
LOG2E = 1.4426950408889634
SCALE = HEAD_DIM ** -0.5
TO_LOG2 = SCALE * LOG2E
BF = jnp.bfloat16
F32 = jnp.float32
MADE = ((0, (0, 0), True), (1, (1, 2), True), (2, (0, 0), False), (3, (0, 0), False), (0, (3, 3), True))
BACK = (0, 2, 3, 1)
AHEAD = (0, 2, 1, 3)
BLOCK = 3 * TOK
NOTE = 16
WIDE = 256
VMEM_LIMIT = 48 * 1024 * 1024
PREP_LIMIT = 213 * 256 * 1024


def tiles(first, second, third, spread):
    parts = []
    for t, block in enumerate((first, second, third)):
        parts.append(jnp.concatenate([block, spread[:, t * TAIL : (t + 1) * TAIL]], axis=1))
    return jnp.concatenate(parts, axis=0)


def prep_kernel(bits, proj, cot, *rest):
    outs = rest[: len(MADE)]
    proj_in, cot_in, sems = rest[len(MADE) :]
    chip = chip_index()
    core = lax.axis_index("seq") & 1
    copies = []
    for e, (step, on, _) in enumerate(MADE):
        head = lax.rem(chip + step, CHIPS)
        rate = lax.rem(lax.axis_index("rate") + jnp.where(core == 0, on[0], on[1]), CHIPS)
        cols = pl.ds(pl.multiple_of(rate * OWN + (head // 2) * TOK, TOK), 2 * TOK)
        copies.append(
            [
                pltpu.make_async_copy(proj.at[:, :, cols], proj_in.at[e], sems.at[e, 0]),
                pltpu.make_async_copy(cot.at[:, cols], cot_in.at[e], sems.at[e, 1]),
            ]
        )
    for pair in copies:
        for copy in pair:
            copy.start()
    note = jnp.full((NOTE, TOK), bits[0].astype(F32), F32).astype(BF)
    for e, (_, _, noted) in enumerate(MADE):
        if noted:
            outs[e][BLOCK:] = note
    for at in range(CHIPS):

        @pl.when(chip == at)
        def _():
            for e, (step, _, _) in enumerate(MADE):
                head = (at + step) % CHIPS
                first = head * HEAD_DIM - head // 2 * TOK
                cols = slice(first, first + HEAD_DIM)
                for copy in copies[e]:
                    copy.wait()
                outs[e][:BLOCK] = tiles(
                    proj_in[e, 0, :, cols], proj_in[e, 1, :, cols], proj_in[e, 2, :, cols], cot_in[e, :, cols]
                )


def chip_index():
    return lax.rem(lax.axis_index("seq") // 2, CHIPS)


def prep(bits, proj, cot):
    hbm = pl.BlockSpec(memory_space=pltpu.HBM)
    return pl.pallas_call(
        prep_kernel,
        out_shape=[jax.ShapeDtypeStruct((BLOCK + NOTE * noted, TOK), BF) for _, _, noted in MADE],
        in_specs=[pl.BlockSpec(memory_space=pltpu.SMEM), hbm, hbm],
        out_specs=[pl.BlockSpec(memory_space=pltpu.VMEM)] * len(MADE),
        scratch_shapes=[
            pltpu.VMEM((len(MADE), 3, TOK, 2 * TOK), BF),
            pltpu.VMEM((len(MADE), TOK, 2 * TOK), BF),
            pltpu.SemaphoreType.DMA((len(MADE), 2)),
        ],
        compiler_params=pltpu.CompilerParams(vmem_limit_bytes=PREP_LIMIT),
        name="prep",
    )(bits, proj, cot)


def near_level(i, j, odd):
    if i == j:
        return 3
    if i % 4 == j % 4:
        return 2
    if j % 4 == (3, 2, 1, 0)[i % 4]:
        return 1 - odd
    if j % 4 == (1, 0, 3, 2)[i % 4]:
        return odd
    return 0


def main_kernel(*rest):
    ins = [rest[AHEAD.index(s % 4) + s // 4 * 4] for s in range(8)]
    outs = rest[8:12]
    qs, ks, vs, ds, bias, st, dp, et, gt, qn, dn, out, gq, gk, gv = rest[12:]
    odd = chip_index() & 1
    nn = (((1,), (0,)), ((), ()))
    nt = (((1,), (1,)), ((), ()))
    tn = (((0,), (0,)), ((), ()))
    lane = lax.broadcasted_iota(jnp.int32, (TOK, TOK), 1)
    for s in range(8):
        rows = pl.ds(s * TOK, TOK)
        block = ins[s]
        qs[rows] = block[:TOK]
        ks[rows] = jnp.where(lane < HEAD_DIM, block[TOK : 2 * TOK], jnp.zeros((), BF))
        vs[rows] = jnp.where(
            lane < HEAD_DIM, block[2 * TOK : BLOCK], jnp.where(lane == HEAD_DIM, jnp.ones((), BF), jnp.zeros((), BF))
        )
        ds[rows] = jnp.concatenate(
            [block[t * TOK : (t + 1) * TOK, HEAD_DIM:] for t in range(3)] + [jnp.zeros((TOK, TAIL), BF)], axis=1
        )
    key = lax.broadcasted_iota(jnp.int32, (8, TOK), 0)
    query = lax.broadcasted_iota(jnp.int32, (8, TOK), 1) & 7
    apart = key ^ query
    count = jnp.zeros((8, TOK), F32)
    noted = [ins[e][BLOCK:].astype(F32)[:8] for e in (0, 1, 4, 5)]
    for level, mask in ((0, 7), (1, 3), (2, 1), (3, 0)):
        rate_bits = 3 - level
        branches = jnp.zeros((8, TOK), F32)
        for b in range(4):
            branches = branches + jnp.where(noted[b] == float(rate_bits), 1.0, 0.0)
        count = count + jnp.where((apart & mask) == 0, branches, 0.0)
        bias[level] = jnp.where(count > 0.0, jnp.log2(jnp.maximum(count, 1.0)) * (1.0 / TO_LOG2), NEG)

    def products(c):
        cols = slice(c * WIDE, (c + 1) * WIDE)
        st[c] = lax.dot_general(ks[...], qs[cols], nt, preferred_element_type=F32)
        keys = slice(0, SEG if c * WIDE < HALF else HALF)
        dp[c, keys] = lax.dot_general(vs[keys], ds[cols], nt, preferred_element_type=F32)

    def weights(c):
        for i in range(c * WIDE // TOK, (c + 1) * WIDE // TOK):
            spot = slice(i * TOK - c * WIDE, (i + 1) * TOK - c * WIDE)
            cols = slice(i * TOK, (i + 1) * TOK)
            near = [bias[near_level(i, j, odd)] for j in range(8)]
            top = None
            for j in range(8):
                rows = slice(j * TOK, (j + 1) * TOK)
                j_top = jnp.max(st[c, rows, spot].reshape(16, 8, TOK) + near[j][None], axis=0)
                top = j_top if top is None else jnp.maximum(top, j_top)
            top = jnp.max(top, axis=0, keepdims=True)
            for j in range(8):
                rows = slice(j * TOK, (j + 1) * TOK)
                t = st[c, rows, spot].reshape(16, 8, TOK) + (near[j] - top)[None]
                et[rows, cols] = jnp.exp2(t * TO_LOG2).reshape(TOK, TOK).astype(BF)

    def scores(c):
        cols = slice(c * WIDE, (c + 1) * WIDE)
        summed = lax.dot_general(vs[...], et[:, cols], tn, preferred_element_type=F32)
        over = 1.0 / summed[HEAD_DIM : HEAD_DIM + 1]
        merged = summed * over
        if c * WIDE < HALF:
            out[cols] = jnp.transpose(merged)
        inner = jnp.sum(merged * jnp.transpose(ds[cols].astype(F32)), axis=0, keepdims=True)
        for i in range(c * WIDE // TOK, (c + 1) * WIDE // TOK):
            spot = slice(i * TOK - c * WIDE, (i + 1) * TOK - c * WIDE)
            cols = slice(i * TOK, (i + 1) * TOK)
            for j in range(4 if i >= 4 else 8):
                rows = slice(j * TOK, (j + 1) * TOK)
                gt[rows, cols] = (et[rows, cols].astype(F32) * (dp[c, rows, spot] - inner[:, spot])).astype(BF)
            upright = jnp.transpose(jnp.broadcast_to(over[:, spot], (TOK, TOK)))
            qn[cols] = (qs[cols].astype(F32) * (upright * SCALE)).astype(BF)
            dn[cols] = (ds[cols].astype(F32) * upright).astype(BF)
        return over

    chunks = SEG // WIDE
    products(0)
    overs = []
    for c in range(chunks):
        if c + 1 < chunks:
            products(c + 1)
        weights(c)
        overs.append(scores(c))
    gv[...] = lax.dot_general(et[:HALF], dn[...], nn, preferred_element_type=F32)
    gk[...] = lax.dot_general(gt[:HALF], qn[...], nn, preferred_element_type=F32)
    part = lax.dot_general(ks[...], gt[:, :HALF], tn, preferred_element_type=F32)
    gq[...] = jnp.transpose(part * (jnp.concatenate(overs[: HALF // WIDE], axis=1) * SCALE))
    made = []
    for d in range(4):
        rows = slice(d * TOK, (d + 1) * TOK)
        made.append(
            tiles(
                out[rows, :HEAD_DIM].astype(BF),
                gq[rows, :HEAD_DIM].astype(BF),
                gk[rows, :HEAD_DIM].astype(BF),
                gv[rows].astype(BF),
            )
        )
    outs[0][...] = made[0]
    outs[1][...] = jnp.where(odd == 1, made[1], made[3])
    outs[2][...] = made[2]
    outs[3][...] = jnp.where(odd == 1, made[3], made[1])


def attend(blocks):
    vmem = pl.BlockSpec(memory_space=pltpu.VMEM)
    return pl.pallas_call(
        main_kernel,
        out_shape=[jax.ShapeDtypeStruct((BLOCK, TOK), BF)] * CHIPS,
        in_specs=[vmem] * 8,
        out_specs=[vmem] * CHIPS,
        scratch_shapes=[pltpu.VMEM((SEG, TOK), BF)] * 4
        + [
            pltpu.VMEM((4, 8, TOK), F32),
            pltpu.VMEM((SEG // WIDE, SEG, WIDE), F32),
            pltpu.VMEM((SEG // WIDE, SEG, WIDE), F32),
            pltpu.VMEM((SEG, SEG), BF),
            pltpu.VMEM((SEG, SEG), BF),
            pltpu.VMEM((SEG, TOK), BF),
            pltpu.VMEM((SEG, TOK), BF),
        ]
        + [pltpu.VMEM((HALF, TOK), F32)] * 4,
        compiler_params=pltpu.CompilerParams(vmem_limit_bytes=VMEM_LIMIT),
        name="attend",
    )(*blocks)


def final_kernel(*rest):
    ins = rest[:4]
    attended, grads, held, sems = rest[4:]
    chip = chip_index()
    copies = [pltpu.make_async_copy(held.at[0], attended, sems.at[0])]
    for t in range(3):
        copies.append(pltpu.make_async_copy(held.at[t + 1], grads.at[t], sems.at[t + 1]))
    for at in range(CHIPS):

        @pl.when(chip == at)
        def _():
            blocks = [ins[BACK.index(h ^ at)] for h in range(CHIPS)]
            for t in range(3):
                held[t] = jnp.concatenate([block[t * TOK : (t + 1) * TOK, :HEAD_DIM] for block in blocks], axis=1)
                copies[t].start()
            held[3] = jnp.concatenate(
                [block[t * TOK : (t + 1) * TOK, HEAD_DIM:] for block in blocks for t in range(3)], axis=1
            )
            copies[3].start()

    for copy in copies:
        copy.wait()


def final(blocks):
    vmem = pl.BlockSpec(memory_space=pltpu.VMEM)
    hbm = pl.BlockSpec(memory_space=pltpu.HBM)
    return pl.pallas_call(
        final_kernel,
        out_shape=[jax.ShapeDtypeStruct((TOK, OWN), BF), jax.ShapeDtypeStruct((3, TOK, OWN), BF)],
        in_specs=[vmem] * 4,
        out_specs=[hbm] * 2,
        scratch_shapes=[pltpu.VMEM((4, TOK, OWN), BF), pltpu.SemaphoreType.DMA((4,))],
        compiler_params=pltpu.CompilerParams(vmem_limit_bytes=VMEM_LIMIT),
        name="final",
    )(*blocks)


def moved(block, chips, flip, rates):
    seq, ring = lax.axis_size("seq"), lax.axis_size("rate")
    pairs = []
    for i in range(seq):
        to = i - i % 8 + ((i // 2 + chips) % CHIPS) * 2 + (i % 2 ^ flip)
        for r in range(ring):
            pairs.append((i * ring + r, to * ring + (r + rates[i % 2]) % ring))
    return lax.ppermute(block, ("seq", "rate"), pairs)


def traded(block, across):
    return lax.ppermute(block, "seq", [(i, i ^ across * 2) for i in range(lax.axis_size("seq"))])


def body(projections, dilation_bits, grad_out):
    sent = prep(dilation_bits, jnp.transpose(projections, (1, 0, 2)), grad_out)
    near = [sent[0]] + [moved(sent[e], MADE[e][0], 0, MADE[e][1]) for e in range(1, CHIPS)]
    far = [moved(sent[CHIPS], 0, 1, MADE[CHIPS][1])] + [moved(block, 0, 1, (0, 0)) for block in near[1:]]
    results = attend([near[d] for d in AHEAD] + [far[d] for d in AHEAD])
    back = [traded(results[k], k) if k else results[k] for k in BACK]
    attended, grads = final(back)
    return attended, jnp.transpose(grads, (1, 0, 2))


def solution(mesh):
    in_specs = (P("seq", None, None), P("rate"), P("seq", None))
    out_specs = (P("seq", "rate"), P("seq", None, "rate"))
    return jax.shard_map(body, mesh=mesh, in_specs=in_specs, out_specs=out_specs, check_vma=False)
```
